512 devices in a mesh: op: 128 (over x_hi, y, z), sec: 4 (over x_lo, core).
Axes of the slice: x: 4 (x_hi: 2, x_lo: 2; x = x_hi * 2 + x_lo), y: 4, z: 16, core: 2. Of those that a mesh axis runs over, the one named last changes fastest.
Arguments:
- wavefunction: float32 [2, 4, 256, 256], P(None, 'sec'), may hold values from -6 to 6
- left_ops: float32 [1024, 4, 256, 256], P('op', 'sec'), may hold values from -0.125 to 0.125
- right_ops: float32 [1024, 4, 256, 256], P('op', 'sec'), may hold values from -0.375 to 0.375
- term_shift: int32 [1024], P('op'), may hold values from -1 to 1
- term_count: int32 [128], P('op'), may hold values from 1 to 8, as said below
- sector_dims: int32 [4], P('sec'), may hold values from 64 to 256, as said below
Outputs:
- sigma: float32 [2, 4, 256, 256], P(None, 'sec', 'op')
The draws below stay inside these ranges and needn't reach their ends.
Inputs may be any that keep to these rules, and one draw needn't show every extreme that they name: `term_count`: live term slots of an index of op are its first ones; some index has all 8 live. `sector_dims`: some sector has the full dimension 256.
All inputs are finite; a program needn't handle non-finite values.
Results may differ from the reference program's by a relative error of at most 0.0003.
Values sent between devices are 32-bit elements; how exact they have to be, the bound alone decides.
A program may use at most 64 MiB of HBM per device.

```python
import jax
import jax.numpy as jnp
from jax import lax

B = 256
VECS = 2
KT = 8
S = 4
TERMS = 1024
N_OP = 128


def draw_term_count(key, part):
    key = jax.random.fold_in(key, 11)
    first_key, second_key = jax.random.split(key)
    counts = jax.random.randint(first_key, (N_OP,), 1, KT + 1)
    full_index = jax.random.randint(second_key, (), 0, N_OP)
    return jnp.where(jnp.arange(N_OP) == full_index, KT, counts).astype(jnp.int32)


def draw_sector_dims(key, part):
    key = jax.random.fold_in(key, 23)
    first_key, second_key = jax.random.split(key)
    dims_drawn = jax.random.randint(first_key, (S,), B // 4, B + 1)
    full_index = jax.random.randint(second_key, (), 0, S)
    return jnp.where(jnp.arange(S) == full_index, B, dims_drawn).astype(jnp.int32)


def touch_ends(result, stream_key, smallest, high):
    spot = [jax.random.randint(jax.random.fold_in(stream_key, axis), (), 0, length) for axis, length in enumerate(result.shape)]
    widest = result.shape.index(max(result.shape))
    beside = spot[:widest] + [(spot[widest] + 1) % result.shape[widest]] + spot[widest + 1:]
    return result.at[tuple(spot)].set(smallest).at[tuple(beside)].set(high)


def strengthened(values, own_key, source, target, blocks, factor):
    owner, partner = [(jnp.arange(values.shape[position]) // (values.shape[position] // blocks)).reshape([-1 if axis == position else 1 for axis in range(values.ndim)]) for position in (source, target)]
    chosen = jax.random.permutation(own_key, blocks)[partner]
    strong = (owner == chosen) | (owner == (partner + blocks // 2) % blocks)
    return jnp.where(strong, factor * values, values)


def shard_levels(stream_key, shape, shards, smallest, largest):
    def one(position, blocks):
        draws = jax.random.uniform(jax.random.fold_in(jax.random.fold_in(stream_key, 6), position), (blocks,), jnp.float32, smallest / len(shards), largest / len(shards))
        return jnp.repeat(jnp.exp(draws), shape[position] // blocks).reshape((-1,) + (1,) * (len(shape) - position - 1))

    level = one(*shards[0])
    for cut in shards[1:]:
        level = level * one(*cut)
    return level


def scatter_about(key, extent, scale, bound, cuts=(), held_as=jnp.bfloat16):
    drawn = jax.random.normal(key, extent, jnp.float32) * scale
    if len(cuts) > 0:
        drawn = shard_levels(key, extent, cuts, -0.22, 0.18) * drawn
    return jnp.clip(drawn, min=-bound, max=bound).astype(held_as)


def heavy_noise(key, extent, spread, reach, shards, heavy, held_as=jnp.bfloat16):
    entries = spread * jax.random.normal(key, extent, jnp.float32)
    if shards:
        entries = entries * shard_levels(key, extent, shards, -0.22, 0.18)
    return jnp.clip(strengthened(entries, jax.random.fold_in(key, 3), *heavy), -reach, reach).astype(held_as)


def setup_inputs(seed: int = 0) -> dict:
    streams_of = jax.random.split(jax.random.key(seed), 7)
    wavefunction = scatter_about(streams_of[0], (VECS, S, B, B), 1.0, 6.0, ((1, 4),), jnp.float32)
    left_ops = heavy_noise(streams_of[1], (TERMS, S, B, B), (B * N_OP) ** -0.5, 0.125, ((0, 128), (1, 4)), (0, 2, 128, 5.5), jnp.float32)
    right_ops = scatter_about(streams_of[2], (TERMS, S, B, B), B ** -0.5, 0.375, ((0, 128), (1, 4)), jnp.float32)
    term_shift = touch_ends(jax.random.randint(streams_of[3], (TERMS,), -1, 2), jax.random.fold_in(streams_of[3], 1), -1, 1).astype(jnp.int32)
    term_count = draw_term_count(jax.random.fold_in(streams_of[6], 71), 0)
    sector_dims = draw_sector_dims(jax.random.fold_in(streams_of[6], 71), 0)
    return {"wavefunction": wavefunction, "left_ops": left_ops, "right_ops": right_ops, "term_shift": term_shift, "term_count": term_count, "sector_dims": sector_dims}


def reference(wavefunction, left_ops, right_ops, term_shift, term_count, sector_dims):
    row_index = jnp.arange(B, dtype=jnp.int32)
    row_mask = (row_index[None, :] < sector_dims[:, None]).astype(jnp.float32)
    masked = wavefunction * row_mask[None, :, :, None]
    padded = jnp.pad(masked, ((0, 0), (1, 1), (0, 0), (0, 0)))
    term_index = jnp.arange(TERMS, dtype=jnp.int32)
    owner_count = term_count[term_index // KT]
    live = ((term_index % KT) < owner_count).astype(jnp.float32)

    def add_term(summed, inputs):
        left_block, right_block, offset, weight = inputs
        source = lax.dynamic_slice_in_dim(padded, (1 - offset).astype(jnp.int32), S, 1)
        half = jnp.einsum("vjab,jcb->vjac", source, right_block, precision=lax.Precision.HIGHEST)
        product = jnp.einsum("jab,vjbc->vjac", left_block, half, precision=lax.Precision.HIGHEST)
        return summed + weight * product, None

    start_value = jnp.zeros((VECS, S, B, B), jnp.float32)
    summed, unused = lax.scan(add_term, start_value, (left_ops, right_ops, term_shift, live))
    return summed * row_mask[None, :, :, None]
```

```python
import jax
import jax.numpy as jnp
from jax import lax
from jax.experimental import pallas as pl
from jax.experimental.pallas import tpu as pltpu
from jax.sharding import PartitionSpec as P

MESH = pl.DeviceIdType.MESH
F32, BF16 = jnp.float32, jnp.bfloat16
XH, Y, Z = 2, 4, 16
VECS, B, KT = 2, 256, 8
OWN = B // (XH * Y)
NEAR = [(a, b) for a in range(XH) for b in range(Y) if (a, b) != (0, 0)]
NN = (((1,), (0,)), ((), ()))
NT = (((1,), (1,)), ((), ()))


def split(x):
    hi = x.astype(BF16)
    return hi, (x - hi.astype(F32)).astype(BF16)


def dot3(ah, al, bh, bl, dims):
    def dot(a, b):
        return lax.dot_general(a, b, dims, preferred_element_type=F32)

    return dot(ah, bh) + dot(ah, bl) + dot(al, bh)


def kernel(
    shift_ref, count_ref, dims_ref, w_hbm, l_hbm, r_hbm, out_ref,
    wv, lv, rv, got, sh, sl, lh, ll, rh, rl, gh, gl, part, near_buf, zsrc, zbuf,
    load_sem, ex_send, ex_recv, near_send, near_recv, z_send, z_recv,
):
    op, sec = lax.axis_index("op"), lax.axis_index("sec")
    xh, y, z = op // (Y * Z), (op // Z) % Y, op % Z

    def place(a, b, c):
        return (a * (Y * Z) + b * Z + c, sec)

    load_w = pltpu.make_async_copy(w_hbm, wv, load_sem.at[0])
    load_l = pltpu.make_async_copy(l_hbm, lv, load_sem.at[1])
    load_r = pltpu.make_async_copy(r_hbm, rv, load_sem.at[2])
    load_w.start()
    load_l.start()
    load_r.start()

    barrier = pltpu.get_barrier_semaphore()
    other_op = (1 - xh) * (Y * Z) + y * Z + z

    def greet(target):
        pl.semaphore_signal(barrier, inc=1, device_id=target, device_id_type=MESH)

    for a, b in NEAR:
        greet(place((xh + a) % XH, (y + b) % Y, z))
    for c in range(1, Z):
        greet(place(xh, y, (z + c) % Z))
    up = jnp.where(sec < 3, sec + 1, sec - 3)
    down = jnp.where(sec > 0, sec - 1, sec + 3)
    for a in (op, other_op):
        greet((a, up))
        greet((a, down))

    load_w.wait()
    rows = dims_ref[0]
    row = lax.broadcasted_iota(jnp.int32, (B, B), 0)
    for v in range(VECS):
        m = jnp.where(row < rows, wv[v], 0.0)
        wv[v] = m
        h, l = split(m)
        sh[1, :, v * B : (v + 1) * B] = h
        sl[1, :, v * B : (v + 1) * B] = l
    sh[3] = jnp.zeros((B, VECS * B), BF16)
    sl[3] = jnp.zeros((B, VECS * B), BF16)

    pl.semaphore_wait(barrier, len(NEAR) + Z - 1 + 4)

    def ways(step):
        cross = (sec == 1) if step == 0 else (sec == 2)
        target = sec + 1 if step == 0 else sec - 1
        second = jnp.where(cross, other_op, op)
        slot = 0 if step == 0 else 1
        copies = []
        for half in range(2):
            for v in range(VECS):
                part_rows = pl.ds(half * (B // 2), B // 2)
                copies.append(
                    pltpu.make_async_remote_copy(
                        src_ref=wv.at[v, part_rows],
                        dst_ref=got.at[slot, v, part_rows],
                        send_sem=ex_send.at[slot, half, v],
                        recv_sem=ex_recv.at[slot, half, v],
                        device_id=(op if half == 0 else second, target),
                        device_id_type=MESH,
                    )
                )
        return copies

    to_next, to_prev = ways(0), ways(1)

    @pl.when(sec < 3)
    def _():
        for c in to_next:
            c.start()

    @pl.when(sec > 0)
    def _():
        for c in to_prev:
            c.start()

    load_l.wait()

    def split_l(t, carry):
        h, l = split(lv[t])
        lh[t] = h
        ll[t] = l
        return carry

    lax.fori_loop(0, KT, split_l, 0)
    load_r.wait()
    for t in range(KT):
        h, l = split(rv[t])
        rh[:, t * B : (t + 1) * B] = h
        rl[:, t * B : (t + 1) * B] = l

    def take(slot, index):
        for v in range(VECS):
            h, l = split(got[slot, v])
            sh[index, :, v * B : (v + 1) * B] = h
            sl[index, :, v * B : (v + 1) * B] = l

    @pl.when(sec > 0)
    def _():
        for c in to_next:
            c.wait_recv()
        take(0, 0)

    @pl.when(sec < 3)
    def _():
        for c in to_prev:
            c.wait_recv()
        take(1, 2)

    half_rows = B // XH
    for t in range(KT):
        s = shift_ref[t]
        at = sec - s
        ok = (t < count_ref[0]) & (at >= 0) & (at <= 3)
        i = jnp.where(ok, 1 - s, 3)
        g = dot3(lh[t], ll[t], sh[i], sl[i], NN)
        h, l = split(g)
        for a in range(XH):
            for v in range(VECS):
                gh[a, v, :, t * B : (t + 1) * B] = h[a * half_rows : (a + 1) * half_rows, v * B : (v + 1) * B]
                gl[a, v, :, t * B : (t + 1) * B] = l[a * half_rows : (a + 1) * half_rows, v * B : (v + 1) * B]

    def near_copy(a, b):
        i = NEAR.index((a, b))
        return pltpu.make_async_remote_copy(
            src_ref=part.at[a, (y + b) % Y],
            dst_ref=near_buf.at[i],
            send_sem=near_send.at[i],
            recv_sem=near_recv.at[i],
            device_id=place((xh + a) % XH, (y + b) % Y, z),
            device_id_type=MESH,
        )

    near = {ab: near_copy(*ab) for ab in NEAR}
    for a in (1, 0):
        which = (xh + a) % XH
        m = VECS * half_rows
        p = dot3(
            gh[which].reshape(m, KT * B), gl[which].reshape(m, KT * B), rh[...], rl[...], NT
        ).reshape(VECS, Y, OWN, B)
        for b in range(Y):
            part[a, b] = p[:, b]
        for b in (2, 1, 3, 0):
            if (a, b) in near:
                near[a, b].start()

    for ab in NEAR:
        near[ab].wait_recv()
    total = part[0, y]
    for i in range(len(NEAR)):
        total = total + near_buf[i]
    for v in range(VECS):
        for rb in range(OWN // 8):
            for ch in range(2):
                zsrc[pl.ds(32 * rb + 2 * v + ch, 8, stride=4), :] = total[v, rb * 8 : rb * 8 + 8, ch * 128 : ch * 128 + 128]

    far = []
    for k in range(1, Z):
        to = (z + k) % Z
        far.append(
            pltpu.make_async_remote_copy(
                src_ref=zsrc.at[pl.ds(pl.multiple_of(to * 8, 8), 8)],
                dst_ref=zbuf.at[pl.ds((k - 1) * 8, 8)],
                send_sem=z_send.at[k - 1],
                recv_sem=z_recv.at[k - 1],
                device_id=place(xh, y, to),
                device_id_type=MESH,
            )
        )
    for k in (8, 7, 9, 6, 10, 5, 11, 4, 12, 3, 13, 2, 14, 1, 15):
        far[k - 1].start()
    for c in far:
        c.wait_recv()
    tile = zsrc[pl.ds(pl.multiple_of(z * 8, 8), 8)]
    for k in range(Z - 1):
        tile = tile + zbuf[k * 8 : k * 8 + 8]
    sub = lax.broadcasted_iota(jnp.int32, (8, 128), 0)
    own_row = 2 * op + jnp.where(sub >= 4, 1, 0)
    tile = jnp.where(own_row < rows, tile, 0.0)
    for s in range(2):
        for v in range(VECS):
            for ch in range(2):
                n = 4 * s + 2 * v + ch
                out_ref[v, 0, s : s + 1, ch * 128 : ch * 128 + 128] = tile[n : n + 1]

    @pl.when(sec < 3)
    def _():
        for c in to_next:
            c.wait_send()

    @pl.when(sec > 0)
    def _():
        for c in to_prev:
            c.wait_send()

    for ab in NEAR:
        near[ab].wait_send()
    for c in far:
        c.wait_send()


def shards(wavefunction, left_ops, right_ops, term_shift, term_count, sector_dims):
    vmem, smem, dma = pltpu.VMEM, pltpu.SMEM, pltpu.SemaphoreType.DMA
    n = len(NEAR)
    return pl.pallas_call(
        kernel,
        out_shape=jax.ShapeDtypeStruct((VECS, 1, 2, B), F32),
        in_specs=[pl.BlockSpec(memory_space=smem)] * 3 + [pl.BlockSpec(memory_space=pl.ANY)] * 3,
        out_specs=pl.BlockSpec(memory_space=vmem),
        scratch_shapes=[
            vmem((VECS, B, B), F32),
            vmem((KT, B, B), F32),
            vmem((KT, B, B), F32),
            vmem((2, VECS, B, B), F32),
            vmem((4, B, VECS * B), BF16),
            vmem((4, B, VECS * B), BF16),
            vmem((KT, B, B), BF16),
            vmem((KT, B, B), BF16),
            vmem((B, KT * B), BF16),
            vmem((B, KT * B), BF16),
            vmem((XH, VECS, B // XH, KT * B), BF16),
            vmem((XH, VECS, B // XH, KT * B), BF16),
            vmem((XH, Y, VECS, OWN, B), F32),
            vmem((n, VECS, OWN, B), F32),
            vmem((Z * 8, 128), F32),
            vmem(((Z - 1) * 8, 128), F32),
            dma((3,)),
            dma((2, 2, VECS)),
            dma((2, 2, VECS)),
            dma((n,)),
            dma((n,)),
            dma((Z - 1,)),
            dma((Z - 1,)),
        ],
        compiler_params=pltpu.CompilerParams(
            collective_id=0, has_side_effects=True, vmem_limit_bytes=56 << 20
        ),
        cost_estimate=pl.CostEstimate(flops=3 * 2**30, bytes_accessed=9 << 19, transcendentals=0),
    )(term_shift, term_count, sector_dims,
      wavefunction.reshape(VECS, B, B), left_ops.reshape(KT, B, B), right_ops.reshape(KT, B, B))


def solution(mesh):
    in_specs = (
        P(None, "sec", None, None),
        P("op", "sec", None, None),
        P("op", "sec", None, None),
        P("op"),
        P("op"),
        P("sec"),
    )
    out_specs = P(None, "sec", "op", None)
    return jax.shard_map(shards, mesh=mesh, in_specs=in_specs, out_specs=out_specs, check_vma=False)
```

```python
import jax
import jax.numpy as jnp
from jax import lax
from jax.experimental import pallas as pl
from jax.experimental.pallas import tpu as pltpu
from jax.sharding import PartitionSpec as P

MESH = pl.DeviceIdType.MESH
F32, BF16 = jnp.float32, jnp.bfloat16
XH, Y, Z = 2, 4, 16
VECS, B, KT = 2, 256, 8
PARTS = 2
CUT = B // (XH * Y * PARTS)
NEAR = [(a, b) for a in range(XH) for b in range(Y) if (a, b) != (0, 0)]
NN = (((1,), (0,)), ((), ()))
NT = (((1,), (1,)), ((), ()))


def split(x):
    hi = x.astype(BF16)
    return hi, (x - hi.astype(F32)).astype(BF16)


def dot(a, b, dims):
    return lax.dot_general(a, b, dims, preferred_element_type=F32)


def kernel(
    shift_hbm, count_hbm, dims_hbm, w_hbm, l_hbm, r_hbm, out_ref,
    shift_ref, count_ref, dims_ref, wv, lv, rv, got, sh, sl, ls, rh, rl, gs, part, near_buf, zsrc, zbuf,
    load_sem, ex_send, ex_recv, near_send, near_recv, z_send, z_recv, know,
):
    op, sec = lax.axis_index("op"), lax.axis_index("sec")
    xh, y, z = op // (Y * Z), (op // Z) % Y, op % Z

    def place(a, b, c):
        return (a * (Y * Z) + b * Z + c, sec)

    def signal(sem, target):
        pl.semaphore_signal(sem, inc=1, device_id=target, device_id_type=MESH)

    barrier = pltpu.get_barrier_semaphore()
    other_op = (1 - xh) * (Y * Z) + y * Z + z
    up = jnp.where(sec < 3, sec + 1, sec - 3)
    down = jnp.where(sec > 0, sec - 1, sec + 3)
    for a in (op, other_op):
        signal(barrier, (a, up))
        signal(barrier, (a, down))
    beside = [place(xh, (y + d) % Y, z) for d in (1, 3)] + [place(xh, y, (z + d) % Z) for d in (1, Z - 1)]
    for target in beside:
        signal(barrier, target)

    loads = [
        pltpu.make_async_copy(s, d, load_sem.at[i])
        for i, (s, d) in enumerate(
            ((dims_hbm, dims_ref), (w_hbm, wv), (l_hbm, lv), (r_hbm, rv), (shift_hbm, shift_ref), (count_hbm, count_ref))
        )
    ]
    for c in loads:
        c.start()

    loads[0].wait()
    loads[1].wait()
    rows = dims_ref[0]
    row = lax.broadcasted_iota(jnp.int32, (B, B), 0)
    for v in range(VECS):
        wv[v] = jnp.where(row < rows, wv[v], 0.0)
    pl.semaphore_wait(barrier, 8)

    def ways(step):
        cross = (sec == 1) if step == 0 else (sec == 2)
        target = sec + 1 if step == 0 else sec - 1
        second = jnp.where(cross, other_op, op)
        slot = 0 if step == 0 else 1
        copies = []
        for v in range(VECS):
            for half in range(2):
                part_rows = pl.ds(half * (B // 2), B // 2)
                copies.append(
                    pltpu.make_async_remote_copy(
                        src_ref=wv.at[v, part_rows],
                        dst_ref=got.at[slot, v, part_rows],
                        send_sem=ex_send.at[slot, half, v],
                        recv_sem=ex_recv.at[slot, half, v],
                        device_id=(op if half == 0 else second, target),
                        device_id_type=MESH,
                    )
                )
        return copies

    to_next, to_prev = ways(0), ways(1)

    @pl.when(sec < 3)
    def _():
        for c in to_next:
            c.start()

    @pl.when(sec > 0)
    def _():
        for c in to_prev:
            c.start()

    for target in beside:
        signal(know.at[0], target)

    for v in range(VECS):
        h, l = split(wv[v])
        sh[v, 1] = h
        sl[v, 1] = l
        sh[v, 3] = jnp.zeros((B, B), BF16)
        sl[v, 3] = jnp.zeros((B, B), BF16)

    loads[2].wait()

    def split_l(t, carry):
        h, l = split(lv[t].reshape(XH * Y, PARTS, CUT, B))
        for c in range(PARTS):
            ls[c, t, : B // PARTS] = h[:, c].reshape(B // PARTS, B)
            ls[c, t, B // PARTS :] = l[:, c].reshape(B // PARTS, B)
        return carry

    lax.fori_loop(0, KT, split_l, 0)
    loads[3].wait()
    for t in range(KT):
        h, l = split(rv[t])
        rh[:, t * B : (t + 1) * B] = h
        rl[:, t * B : (t + 1) * B] = l

    pl.semaphore_wait(know.at[0], 4)
    for d in (2, Z - 2):
        signal(know.at[1], place(xh, y, (z + d) % Z))

    loads[4].wait()
    loads[5].wait()
    index = []
    for t in range(KT):
        s = shift_ref[t]
        at = sec - s
        ok = (t < count_ref[0]) & (at >= 0) & (at <= 3)
        index.append(jnp.where(ok, 1 - s, 3))

    m = B // PARTS

    def left(c, v):
        for t in range(KT):
            i = index[t]
            g = dot(ls[c, t], sh[v, i], NN)
            h, l = split(g[:m] + g[m:] + dot(ls[c, t, :m], sl[v, i], NN))
            gs[c, 0, v, :, t * B : (t + 1) * B] = h
            gs[c, 1, v, :, t * B : (t + 1) * B] = l

    for v in range(VECS):
        for copies, edge, slot, i in ((to_next, sec > 0, 0, 0), (to_prev, sec < 3, 1, 2)):

            @pl.when(edge)
            def _():
                for c in copies[2 * v : 2 * v + 2]:
                    c.wait_recv()
                h, l = split(got[slot, v])
                sh[v, i] = h
                sl[v, i] = l

        if v == VECS - 1:
            for d in (1, 2, 3):
                signal(know.at[2], place(xh, (y + d) % Y, z))
            pl.semaphore_wait(know.at[1], 2)
            for d in (4, Z - 4):
                signal(know.at[3], place(xh, y, (z + d) % Z))
        left(0, v)

    def near_copy(c, a, b):
        i = NEAR.index((a, b))
        to = (xh + a) % XH * Y + (y + b) % Y
        return pltpu.make_async_remote_copy(
            src_ref=part.at[c, to],
            dst_ref=near_buf.at[c, i],
            send_sem=near_send.at[c, i],
            recv_sem=near_recv.at[c, i],
            device_id=(to * Z + z, sec),
            device_id_type=MESH,
        )

    def right(c):
        hi = gs[c].reshape(2 * VECS * m, KT * B)
        p = dot(hi, rh[...], NT)
        n = VECS * m
        p = (p[:n] + p[n:] + dot(gs[c, 0].reshape(n, KT * B), rl[...], NT)).reshape(VECS, XH * Y, CUT, B)
        for q in range(XH * Y):
            part[c, q] = p[:, q]

    near = [[near_copy(c, a, b) for a, b in NEAR] for c in range(PARTS)]
    for c in range(PARTS):
        if c > 0:
            for v in range(VECS):
                left(c, v)
        right(c)
        if c == 0:
            pl.semaphore_wait(know.at[2], 3)
        for a, b in ((1, 2), (1, 1), (1, 3), (1, 0), (0, 2), (0, 1), (0, 3)):
            near[c][NEAR.index((a, b))].start()

    per = Z // PARTS

    def far_copy(c, j):
        to = c * per + j
        slot = (to - z + Z) % Z - 1
        slot = jnp.where(slot < 0, 0, slot)
        return pltpu.make_async_remote_copy(
            src_ref=zsrc.at[c, pl.ds(j * 8, 8)],
            dst_ref=zbuf.at[slot],
            send_sem=z_send.at[to],
            recv_sem=z_recv.at[slot],
            device_id=place(xh, y, to),
            device_id_type=MESH,
        )

    for c in range(PARTS):
        for n in near[c]:
            n.wait_recv()
        total = part[c, xh * Y + y]
        for i in range(len(NEAR)):
            total = total + near_buf[c, i]
        for v in range(VECS):
            for rb in range(CUT // 8):
                for ch in range(2):
                    zsrc[c, pl.ds(32 * rb + 2 * v + ch, 8, stride=4), :] = total[
                        v, rb * 8 : rb * 8 + 8, ch * 128 : ch * 128 + 128
                    ]
        if c == 0:
            pl.semaphore_wait(know.at[3], 2)
        for j in range(per):

            @pl.when(c * per + j != z)
            def _():
                far_copy(c, j).start()

    for k in range(Z - 1):
        pltpu.make_async_remote_copy(
            src_ref=zsrc.at[0, pl.ds(0, 8)],
            dst_ref=zbuf.at[k],
            send_sem=z_send.at[0],
            recv_sem=z_recv.at[k],
            device_id=place(xh, y, (z + 1) % Z),
            device_id_type=MESH,
        ).wait_recv()
    tile = zsrc[z // per, pl.ds(pl.multiple_of(z % per * 8, 8), 8)]
    for k in range(Z - 1):
        tile = tile + zbuf[k]
    sub = lax.broadcasted_iota(jnp.int32, (8, 128), 0)
    own_row = 2 * op + jnp.where(sub >= 4, 1, 0)
    tile = jnp.where(own_row < rows, tile, 0.0)
    for s in range(2):
        out_ref[pl.ds(s, 4, stride=2), :] = tile[4 * s : 4 * s + 4]

    @pl.when(sec < 3)
    def _():
        for c in to_next:
            c.wait_send()

    @pl.when(sec > 0)
    def _():
        for c in to_prev:
            c.wait_send()

    for c in range(PARTS):
        for n in near[c]:
            n.wait_send()
        for j in range(per):

            @pl.when(c * per + j != z)
            def _():
                far_copy(c, j).wait_send()


def shards(wavefunction, left_ops, right_ops, term_shift, term_count, sector_dims):
    vmem, smem, dma = pltpu.VMEM, pltpu.SMEM, pltpu.SemaphoreType.DMA
    n = len(NEAR)
    out = pl.pallas_call(
        kernel,
        out_shape=jax.ShapeDtypeStruct((8, 128), F32),
        in_specs=[pl.BlockSpec(memory_space=pltpu.HBM)] * 3 + [pl.BlockSpec(memory_space=pl.ANY)] * 3,
        out_specs=pl.BlockSpec(memory_space=vmem),
        scratch_shapes=[
            smem((KT,), jnp.int32),
            smem((1,), jnp.int32),
            smem((1,), jnp.int32),
            vmem((VECS, B, B), F32),
            vmem((KT, B, B), F32),
            vmem((KT, B, B), F32),
            vmem((2, VECS, B, B), F32),
            vmem((VECS, 4, B, B), BF16),
            vmem((VECS, 4, B, B), BF16),
            vmem((PARTS, KT, 2 * B // PARTS, B), BF16),
            vmem((B, KT * B), BF16),
            vmem((B, KT * B), BF16),
            vmem((PARTS, 2, VECS, B // PARTS, KT * B), BF16),
            vmem((PARTS, XH * Y, VECS, CUT, B), F32),
            vmem((PARTS, n, VECS, CUT, B), F32),
            vmem((PARTS, Z * 8 // PARTS, 128), F32),
            vmem((Z - 1, 8, 128), F32),
            dma((6,)),
            dma((2, 2, VECS)),
            dma((2, 2, VECS)),
            dma((PARTS, n)),
            dma((PARTS, n)),
            dma((Z,)),
            dma((Z - 1,)),
            pltpu.SemaphoreType.REGULAR((4,)),
        ],
        compiler_params=pltpu.CompilerParams(
            collective_id=0, has_side_effects=True, vmem_limit_bytes=56 << 20
        ),
        cost_estimate=pl.CostEstimate(flops=3 * 2**30, bytes_accessed=9 << 19, transcendentals=0),
    )(term_shift, term_count, sector_dims,
      wavefunction.reshape(VECS, B, B), left_ops.reshape(KT, B, B), right_ops.reshape(KT, B, B))
    return out.reshape(VECS, 2, 2, 128).transpose(0, 2, 1, 3).reshape(VECS, 1, 2, B)


def solution(mesh):
    in_specs = (
        P(None, "sec", None, None),
        P("op", "sec", None, None),
        P("op", "sec", None, None),
        P("op"),
        P("op"),
        P("sec"),
    )
    out_specs = P(None, "sec", "op", None)
    return jax.shard_map(shards, mesh=mesh, in_specs=in_specs, out_specs=out_specs, check_vma=False)
```

```python
import jax
import jax.numpy as jnp
from jax import lax
from jax.experimental import pallas as pl
from jax.experimental.pallas import tpu as pltpu
from jax.sharding import PartitionSpec as P

MESH = pl.DeviceIdType.MESH
F32, BF16 = jnp.float32, jnp.bfloat16
XH, Y, Z = 2, 4, 16
VECS, B, KT = 2, 256, 8
HUB = 4
ENDS = (0, 4, 8, 16)
PARTS = len(ENDS) - 1
CUT = [2 * (b - a) for a, b in zip(ENDS, ENDS[1:])]
ROWS = [XH * Y * n for n in CUT]
NEAR = [(a, b) for a in range(XH) for b in range(Y) if (a, b) != (0, 0)]
NN = (((1,), (0,)), ((), ()))


def split(x):
    hi = x.astype(BF16)
    return hi, (x - hi.astype(F32)).astype(BF16)


def dot(a, b, dims):
    return lax.dot_general(a, b, dims, preferred_element_type=F32)


def kernel(
    shift_hbm, count_hbm, dims_hbm, w_hbm, l_hbm, r_hbm, out_ref,
    shift_ref, count_ref, dims_ref, wv, lv, rv, got, sh, sl, ls, rh, rl, gs, part, near_buf, zsrc, zbuf,
    load_sem, ex_send, ex_recv, near_send, near_recv, z_send, z_recv, know,
):
    op, sec = lax.axis_index("op"), lax.axis_index("sec")
    xh, y, z = op // (Y * Z), (op // Z) % Y, op % Z

    def place(a, b, c):
        return (a * (Y * Z) + b * Z + c, sec)

    def signal(sem, target):
        pl.semaphore_signal(sem, inc=1, device_id=target, device_id_type=MESH)

    loads = [
        pltpu.make_async_copy(s, d, load_sem.at[i])
        for i, (s, d) in enumerate(
            ((dims_hbm, dims_ref), (w_hbm, wv), (l_hbm, lv), (r_hbm, rv), (shift_hbm, shift_ref), (count_hbm, count_ref))
        )
    ]
    loads[0].start()
    loads[1].start()

    barrier = pltpu.get_barrier_semaphore()
    other_op = (1 - xh) * (Y * Z) + y * Z + z
    up = jnp.where(sec < 3, sec + 1, sec - 3)
    down = jnp.where(sec > 0, sec - 1, sec + 3)
    for a in (op, other_op):
        signal(barrier, (a, up))
        signal(barrier, (a, down))
    beside = [place(xh, (y + d) % Y, z) for d in (1, 3)]
    for target in beside:
        signal(barrier, target)

    @pl.when(z < HUB)
    def _():
        for d in range(1, Z):

            @pl.when(z + d < Z)
            def _():
                signal(barrier, place(xh, y, (z + d) % Z))

    loads[0].wait()
    loads[1].wait()
    rows = dims_ref[0]
    row = lax.broadcasted_iota(jnp.int32, (B, B), 0)
    for v in range(VECS):
        wv[v] = jnp.where(row < rows, wv[v], 0.0)
    for i in (2, 3, 4, 5):
        loads[i].start()
    pl.semaphore_wait(barrier, 6 + jnp.where(z < HUB, z, HUB))

    def ways(step):
        cross = (sec == 1) if step == 0 else (sec == 2)
        target = sec + 1 if step == 0 else sec - 1
        second = jnp.where(cross, other_op, op)
        slot = 0 if step == 0 else 1
        copies = []
        for v in range(VECS):
            for half in range(2):
                part_rows = pl.ds(half * (B // 2), B // 2)
                copies.append(
                    pltpu.make_async_remote_copy(
                        src_ref=wv.at[v, part_rows],
                        dst_ref=got.at[slot, v, part_rows],
                        send_sem=ex_send.at[slot, half, v],
                        recv_sem=ex_recv.at[slot, half, v],
                        device_id=(op if half == 0 else second, target),
                        device_id_type=MESH,
                    )
                )
        return copies

    to_next, to_prev = ways(0), ways(1)

    @pl.when(sec < 3)
    def _():
        for c in to_next:
            c.start()

    @pl.when(sec > 0)
    def _():
        for c in to_prev:
            c.start()

    for target in beside:
        signal(know.at[0], target)
    for d in range(HUB):

        @pl.when(z >= HUB)
        def _():
            signal(know.at[1], place(xh, y, d))

        @pl.when((z < HUB) & (d < z))
        def _():
            signal(know.at[2], place(xh, y, d))

    for v in range(VECS):
        h, l = split(wv[v])
        sh[v, 1] = h
        sl[v, 1] = l
        sh[v, 3] = jnp.zeros((B, B), BF16)
        sl[v, 3] = jnp.zeros((B, B), BF16)

    loads[2].wait()

    def split_l(t, carry):
        x = lv[t].reshape(XH * Y, 2 * Z, B)
        for c in range(PARTS):
            h, l = split(x[:, 2 * ENDS[c] : 2 * ENDS[c + 1]].reshape(ROWS[c], B))
            ls[c][t, : ROWS[c]] = h
            ls[c][t, ROWS[c] :] = l
        return carry

    lax.fori_loop(0, KT, split_l, 0)
    loads[3].wait()
    for t in range(KT):
        h, l = split(rv[t].T)
        rh[t] = h
        rl[t] = l

    loads[4].wait()
    loads[5].wait()
    index = []
    for t in range(KT):
        s = shift_ref[t]
        at = sec - s
        ok = (t < count_ref[0]) & (at >= 0) & (at <= 3)
        index.append(jnp.where(ok, 1 - s, 3))

    def slab(c, v, i):
        return (v, i) if c == 0 else (i, v)

    def left(c, v):
        m = ROWS[c]
        for t in range(KT):
            i = index[t]
            g = dot(ls[c][t], sh[v, i], NN)
            h, l = split(g[:m] + g[m:] + dot(ls[c][t, :m], sl[v, i], NN))
            gs[c][(*slab(c, v, 0), slice(None), slice(t * B, (t + 1) * B))] = h
            gs[c][(*slab(c, v, 1), slice(None), slice(t * B, (t + 1) * B))] = l

    def right(c, vs):
        n = len(vs) * ROWS[c]
        both = gs[c][vs[0]] if len(vs) == 1 else gs[c][...]
        p = dot(both.reshape(2 * n, KT * B), rh[...].reshape(KT * B, B), NN)
        p = p[:n] + p[n:] + dot(both[0].reshape(n, KT * B), rl[...].reshape(KT * B, B), NN)
        p = p.reshape(len(vs), XH * Y, CUT[c], B)
        for k, v in enumerate(vs):
            for q in range(XH * Y):
                part[c][q, v] = p[k, q]

    for v in range(VECS):
        for copies, edge, slot, i in ((to_next, sec > 0, 0, 0), (to_prev, sec < 3, 1, 2)):

            @pl.when(edge)
            def _():
                for c in copies[2 * v : 2 * v + 2]:
                    c.wait_recv()
                h, l = split(got[slot, v])
                sh[v, i] = h
                sl[v, i] = l

        if v == 0:
            pl.semaphore_wait(know.at[0], 2)
            for d in (1, 2, 3):
                signal(know.at[3], place(xh, (y + d) % Y, z))
        left(0, v)
        right(0, (v,))

    def near_copy(c, a, b):
        i = NEAR.index((a, b))
        to = (xh + a) % XH * Y + (y + b) % Y
        return pltpu.make_async_remote_copy(
            src_ref=part[c].at[to],
            dst_ref=near_buf[c].at[i],
            send_sem=near_send.at[c, i],
            recv_sem=near_recv.at[c, i],
            device_id=(to * Z + z, sec),
            device_id_type=MESH,
        )

    near = [[near_copy(c, a, b) for a, b in NEAR] for c in range(PARTS)]
    for c in range(PARTS):
        if c > 0:
            for v in range(VECS):
                left(c, v)
            right(c, (0, 1))
        if c == 0:
            pl.semaphore_wait(know.at[3], 3)
        for a, b in ((1, 2), (1, 1), (1, 3), (1, 0), (0, 2), (0, 1), (0, 3)):
            near[c][NEAR.index((a, b))].start()

    def far_copy(c, j):
        to = ENDS[c] + j
        slot = (to - z + Z) % Z - 1
        slot = jnp.where(slot < 0, 0, slot)
        return pltpu.make_async_remote_copy(
            src_ref=zsrc.at[c, pl.ds(j * 8, 8)],
            dst_ref=zbuf.at[slot],
            send_sem=z_send.at[to],
            recv_sem=z_recv.at[slot],
            device_id=place(xh, y, to),
            device_id_type=MESH,
        )

    for c in range(PARTS):
        for n in near[c]:
            n.wait_recv()
        total = part[c][xh * Y + y]
        for i in range(len(NEAR)):
            total = total + near_buf[c][i]
        for v in range(VECS):
            for rb in range(CUT[c] // 8):
                for ch in range(2):
                    zsrc[c, pl.ds(32 * rb + 2 * v + ch, 8, stride=4), :] = total[
                        v, rb * 8 : rb * 8 + 8, ch * 128 : ch * 128 + 128
                    ]
        if c == 0:

            @pl.when(z < HUB - 1)
            def _():
                pl.semaphore_wait(know.at[2], HUB - 1 - z)

        if c == 1:

            @pl.when(z < HUB)
            def _():
                pl.semaphore_wait(know.at[1], Z - HUB)
                for d in range(HUB, Z, HUB):
                    signal(know.at[4], place(xh, y, z + d))

            @pl.when(z >= HUB)
            def _():
                pl.semaphore_wait(know.at[4], 1)

        for j in range(ENDS[c + 1] - ENDS[c]):

            @pl.when(ENDS[c] + j != z)
            def _():
                far_copy(c, j).start()

    for k in range(Z - 1):
        pltpu.make_async_remote_copy(
            src_ref=zsrc.at[0, pl.ds(0, 8)],
            dst_ref=zbuf.at[k],
            send_sem=z_send.at[0],
            recv_sem=z_recv.at[k],
            device_id=place(xh, y, (z + 1) % Z),
            device_id_type=MESH,
        ).wait_recv()
    mine, first = 0, 0
    for c in range(1, PARTS):
        mine = jnp.where(z >= ENDS[c], c, mine)
        first = jnp.where(z >= ENDS[c], ENDS[c], first)
    tile = zsrc[mine, pl.ds(pl.multiple_of((z - first) * 8, 8), 8)]
    for k in range(Z - 1):
        tile = tile + zbuf[k]
    sub = lax.broadcasted_iota(jnp.int32, (8, 128), 0)
    own_row = 2 * op + jnp.where(sub >= 4, 1, 0)
    tile = jnp.where(own_row < rows, tile, 0.0)
    for s in range(2):
        out_ref[pl.ds(s, 4, stride=2), :] = tile[4 * s : 4 * s + 4]

    @pl.when(sec < 3)
    def _():
        for c in to_next:
            c.wait_send()

    @pl.when(sec > 0)
    def _():
        for c in to_prev:
            c.wait_send()

    for c in range(PARTS):
        for n in near[c]:
            n.wait_send()
        for j in range(ENDS[c + 1] - ENDS[c]):

            @pl.when(ENDS[c] + j != z)
            def _():
                far_copy(c, j).wait_send()


def shards(wavefunction, left_ops, right_ops, term_shift, term_count, sector_dims):
    vmem, smem, dma = pltpu.VMEM, pltpu.SMEM, pltpu.SemaphoreType.DMA
    n = len(NEAR)
    out = pl.pallas_call(
        kernel,
        out_shape=vmem((8, 128), F32),
        in_specs=[pl.BlockSpec(memory_space=pltpu.HBM)] * 3 + [pl.BlockSpec(memory_space=pl.ANY)] * 3,
        out_specs=pl.BlockSpec(memory_space=vmem),
        scratch_shapes=[
            smem((KT,), jnp.int32),
            smem((1,), jnp.int32),
            smem((1,), jnp.int32),
            vmem((VECS, B, B), F32),
            vmem((KT, B, B), F32),
            vmem((KT, B, B), F32),
            vmem((2, VECS, B, B), F32),
            vmem((VECS, 4, B, B), BF16),
            vmem((VECS, 4, B, B), BF16),
            [vmem((KT, 2 * m, B), BF16) for m in ROWS],
            vmem((KT, B, B), BF16),
            vmem((KT, B, B), BF16),
            [vmem((2, 2, m, KT * B), BF16) for m in ROWS],
            [vmem((XH * Y, VECS, m, B), F32) for m in CUT],
            [vmem((n, VECS, m, B), F32) for m in CUT],
            vmem((PARTS, 4 * max(CUT), 128), F32),
            vmem((Z - 1, 8, 128), F32),
            dma((6,)),
            dma((2, 2, VECS)),
            dma((2, 2, VECS)),
            dma((PARTS, n)),
            dma((PARTS, n)),
            dma((Z,)),
            dma((Z - 1,)),
            pltpu.SemaphoreType.REGULAR((5,)),
        ],
        compiler_params=pltpu.CompilerParams(
            collective_id=0, has_side_effects=True, vmem_limit_bytes=56 << 20
        ),
        cost_estimate=pl.CostEstimate(flops=3 * 2**30, bytes_accessed=9 << 19, transcendentals=0),
    )(term_shift, term_count, sector_dims,
      wavefunction.reshape(VECS, B, B), left_ops.reshape(KT, B, B), right_ops.reshape(KT, B, B))
    return out.reshape(VECS, 2, 2, 128).transpose(0, 2, 1, 3).reshape(VECS, 1, 2, B)


def solution(mesh):
    in_specs = (
        P(None, "sec", None, None),
        P("op", "sec", None, None),
        P("op", "sec", None, None),
        P("op"),
        P("op"),
        P("sec"),
    )
    out_specs = P(None, "sec", "op", None)
    return jax.shard_map(shards, mesh=mesh, in_specs=in_specs, out_specs=out_specs, check_vma=False)
```

```python
import jax
import jax.numpy as jnp
from jax import lax
from jax.experimental import pallas as pl
from jax.experimental.pallas import tpu as pltpu
from jax.sharding import PartitionSpec as P

MESH = pl.DeviceIdType.MESH
F32, BF16 = jnp.float32, jnp.bfloat16
XH, Y, Z = 2, 4, 16
VECS, B, KT = 2, 256, 8
HUB = 4
ENDS = (0, 4, 8, 16)
PARTS = len(ENDS) - 1
CUT = [2 * (b - a) for a, b in zip(ENDS, ENDS[1:])]
ROWS = [XH * Y * n for n in CUT]
NEAR = [(a, b) for a in range(XH) for b in range(Y) if (a, b) != (0, 0)]
NN = (((1,), (0,)), ((), ()))


def split(x):
    hi = x.astype(BF16)
    return hi, (x - hi.astype(F32)).astype(BF16)


def dot(a, b, dims):
    return lax.dot_general(a, b, dims, preferred_element_type=F32)


def kernel(
    shift_hbm, count_hbm, dims_hbm, w_hbm, l_hbm, r_hbm, out_ref,
    shift_ref, count_ref, dims_ref, wv, lv, rv, got, sh, sl, ls, rh, rl, gs, part, near_buf, zsrc, zbuf,
    load_sem, ex_send, ex_recv, near_send, near_recv, z_sem, know,
):
    op, sec = lax.axis_index("op"), lax.axis_index("sec")
    xh, y, z = op // (Y * Z), (op // Z) % Y, op % Z

    def place(a, b, c):
        return (a * (Y * Z) + b * Z + c, sec)

    def signal(sem, target):
        pl.semaphore_signal(sem, inc=1, device_id=target, device_id_type=MESH)

    loads = [
        pltpu.make_async_copy(s, d, load_sem.at[i])
        for i, (s, d) in enumerate(
            ((dims_hbm, dims_ref), (w_hbm, wv), (l_hbm, lv), (r_hbm, rv), (shift_hbm, shift_ref), (count_hbm, count_ref))
        )
    ]
    loads[0].start()
    loads[1].start()

    barrier = pltpu.get_barrier_semaphore()
    other_op = (1 - xh) * (Y * Z) + y * Z + z
    up = jnp.where(sec < 3, sec + 1, sec - 3)
    down = jnp.where(sec > 0, sec - 1, sec + 3)
    for a in (op, other_op):
        signal(barrier, (a, up))
        signal(barrier, (a, down))
    beside = [place(xh, (y + d) % Y, z) for d in (1, 3)]
    for target in beside:
        signal(barrier, target)

    @pl.when(z < HUB)
    def _():
        for d in range(1, Z):

            @pl.when(z + d < Z)
            def _():
                signal(barrier, place(xh, y, (z + d) % Z))

    loads[0].wait()
    loads[1].wait()
    rows = dims_ref[0]
    row = lax.broadcasted_iota(jnp.int32, (B, B), 0)
    for v in range(VECS):
        wv[v] = jnp.where(row < rows, wv[v], 0.0)
    for i in (2, 3, 4, 5):
        loads[i].start()
    pl.semaphore_wait(barrier, 6 + jnp.where(z < HUB, z, HUB))

    def arrived(ref, sem):
        pltpu.make_async_copy(ref, ref, sem).wait()

    def ways(step):
        cross = (sec == 1) if step == 0 else (sec == 2)
        target = sec + 1 if step == 0 else sec - 1
        second = jnp.where(cross, other_op, op)
        slot = 0 if step == 0 else 1
        copies = []
        for v in range(VECS):
            for half in range(2):
                part_rows = pl.ds(half * (B // 2), B // 2)
                copies.append(
                    pltpu.make_async_remote_copy(
                        src_ref=wv.at[v, part_rows],
                        dst_ref=got.at[slot, v, part_rows],
                        send_sem=ex_send.at[slot, v],
                        recv_sem=ex_recv.at[slot, v],
                        device_id=(op if half == 0 else second, target),
                        device_id_type=MESH,
                    )
                )
        return copies

    to_next, to_prev = ways(0), ways(1)

    @pl.when(sec < 3)
    def _():
        for c in to_next:
            c.start()

    @pl.when(sec > 0)
    def _():
        for c in to_prev:
            c.start()

    for target in beside:
        signal(know.at[0], target)
    for d in range(HUB):

        @pl.when(z >= HUB)
        def _():
            signal(know.at[1], place(xh, y, d))

        @pl.when((z < HUB) & (d < z))
        def _():
            signal(know.at[2], place(xh, y, d))

    for v in range(VECS):
        h, l = split(wv[v])
        sh[v, 1] = h
        sl[v, 1] = l
        sh[v, 3] = jnp.zeros((B, B), BF16)
        sl[v, 3] = jnp.zeros((B, B), BF16)

    loads[2].wait()

    def split_l(t, carry):
        x = lv[t].reshape(XH * Y, 2 * Z, B)
        for c in range(PARTS):
            h, l = split(x[:, 2 * ENDS[c] : 2 * ENDS[c + 1]].reshape(ROWS[c], B))
            ls[c][t, : ROWS[c]] = h
            ls[c][t, ROWS[c] :] = l
        return carry

    lax.fori_loop(0, KT, split_l, 0)
    loads[3].wait()
    for t in range(KT):
        h, l = split(rv[t].T)
        rh[t] = h
        rl[t] = l

    loads[4].wait()
    loads[5].wait()
    index = []
    for t in range(KT):
        s = shift_ref[t]
        at = sec - s
        ok = (t < count_ref[0]) & (at >= 0) & (at <= 3)
        index.append(jnp.where(ok, 1 - s, 3))

    def slab(c, v, i):
        return (v, i) if c == 0 else (i, v)

    def left(c, v):
        m = ROWS[c]
        for t in range(KT):
            i = index[t]
            g = dot(ls[c][t], sh[v, i], NN)
            h, l = split(g[:m] + g[m:] + dot(ls[c][t, :m], sl[v, i], NN))
            gs[c][(*slab(c, v, 0), slice(None), slice(t * B, (t + 1) * B))] = h
            gs[c][(*slab(c, v, 1), slice(None), slice(t * B, (t + 1) * B))] = l

    def right(c, vs):
        n = len(vs) * ROWS[c]
        both = gs[c][vs[0]] if len(vs) == 1 else gs[c][...]
        p = dot(both.reshape(2 * n, KT * B), rh[...].reshape(KT * B, B), NN)
        p = p[:n] + p[n:] + dot(both[0].reshape(n, KT * B), rl[...].reshape(KT * B, B), NN)
        p = p.reshape(len(vs), XH * Y, CUT[c], B)
        for k, v in enumerate(vs):
            for q in range(XH * Y):
                part[c][q, v] = p[k, q]

    for v in range(VECS):
        for edge, slot, i in ((sec > 0, 0, 0), (sec < 3, 1, 2)):

            @pl.when(edge)
            def _():
                arrived(got.at[slot, v], ex_recv.at[slot, v])
                h, l = split(got[slot, v])
                sh[v, i] = h
                sl[v, i] = l

        if v == 0:
            pl.semaphore_wait(know.at[0], 2)
            for d in (1, 2, 3):
                signal(know.at[3], place(xh, (y + d) % Y, z))
        left(0, v)
        right(0, (v,))

    def near_copy(c, a, b):
        i = NEAR.index((a, b))
        to = (xh + a) % XH * Y + (y + b) % Y
        return pltpu.make_async_remote_copy(
            src_ref=part[c].at[to],
            dst_ref=near_buf[c].at[i],
            send_sem=near_send.at[c],
            recv_sem=near_recv.at[c],
            device_id=(to * Z + z, sec),
            device_id_type=MESH,
        )

    near = [[near_copy(c, a, b) for a, b in NEAR] for c in range(PARTS)]
    for c in range(PARTS):
        if c > 0:
            for v in range(VECS):
                left(c, v)
            right(c, (0, 1))
        if c == 0:
            pl.semaphore_wait(know.at[3], 3)
        for a, b in ((1, 2), (1, 1), (1, 3), (1, 0), (0, 2), (0, 1), (0, 3)):
            near[c][NEAR.index((a, b))].start()

    def far_copy(c, j):
        to = ENDS[c] + j
        slot = (to - z + Z) % Z - 1
        slot = jnp.where(slot < 0, 0, slot)
        return pltpu.make_async_remote_copy(
            src_ref=zsrc.at[c, pl.ds(j * 8, 8)],
            dst_ref=zbuf.at[slot],
            send_sem=z_sem.at[0],
            recv_sem=z_sem.at[1],
            device_id=place(xh, y, to),
            device_id_type=MESH,
        )

    for c in range(PARTS):
        arrived(near_buf[c], near_recv.at[c])
        total = part[c][xh * Y + y]
        for i in range(len(NEAR)):
            total = total + near_buf[c][i]
        for v in range(VECS):
            for rb in range(CUT[c] // 8):
                for ch in range(2):
                    zsrc[c, pl.ds(32 * rb + 2 * v + ch, 8, stride=4), :] = total[
                        v, rb * 8 : rb * 8 + 8, ch * 128 : ch * 128 + 128
                    ]
        if c == 0:

            @pl.when(z < HUB - 1)
            def _():
                pl.semaphore_wait(know.at[2], HUB - 1 - z)

        if c == 1:

            @pl.when(z < HUB)
            def _():
                pl.semaphore_wait(know.at[1], Z - HUB)
                for d in range(HUB, Z, HUB):
                    signal(know.at[4], place(xh, y, z + d))

            @pl.when(z >= HUB)
            def _():
                pl.semaphore_wait(know.at[4], 1)

        for j in range(ENDS[c + 1] - ENDS[c]):

            @pl.when(ENDS[c] + j != z)
            def _():
                far_copy(c, j).start()

    @pl.when(sec < 3)
    def _():
        for v in range(VECS):
            arrived(wv.at[v], ex_send.at[0, v])

    @pl.when(sec > 0)
    def _():
        for v in range(VECS):
            arrived(wv.at[v], ex_send.at[1, v])

    for c in range(PARTS):
        arrived(near_buf[c], near_send.at[c])
    arrived(zbuf, z_sem.at[0])

    mine, first = 0, 0
    for c in range(1, PARTS):
        mine = jnp.where(z >= ENDS[c], c, mine)
        first = jnp.where(z >= ENDS[c], ENDS[c], first)
    tile = zsrc[mine, pl.ds(pl.multiple_of((z - first) * 8, 8), 8)]
    sub = lax.broadcasted_iota(jnp.int32, (8, 128), 0)
    own_row = 2 * op + jnp.where(sub >= 4, 1, 0)
    arrived(zbuf, z_sem.at[1])
    for k in range(Z - 1):
        tile = tile + zbuf[k]
    tile = jnp.where(own_row < rows, tile, 0.0)
    for s in range(2):
        out_ref[pl.ds(s, 4, stride=2), :] = tile[4 * s : 4 * s + 4]


def shards(wavefunction, left_ops, right_ops, term_shift, term_count, sector_dims):
    vmem, smem, dma = pltpu.VMEM, pltpu.SMEM, pltpu.SemaphoreType.DMA
    n = len(NEAR)
    out = pl.pallas_call(
        kernel,
        out_shape=vmem((8, 128), F32),
        in_specs=[pl.BlockSpec(memory_space=pltpu.HBM)] * 3 + [pl.BlockSpec(memory_space=pl.ANY)] * 3,
        out_specs=pl.BlockSpec(memory_space=vmem),
        scratch_shapes=[
            smem((KT,), jnp.int32),
            smem((1,), jnp.int32),
            smem((1,), jnp.int32),
            vmem((VECS, B, B), F32),
            vmem((KT, B, B), F32),
            vmem((KT, B, B), F32),
            vmem((2, VECS, B, B), F32),
            vmem((VECS, 4, B, B), BF16),
            vmem((VECS, 4, B, B), BF16),
            [vmem((KT, 2 * m, B), BF16) for m in ROWS],
            vmem((KT, B, B), BF16),
            vmem((KT, B, B), BF16),
            [vmem((2, 2, m, KT * B), BF16) for m in ROWS],
            [vmem((XH * Y, VECS, m, B), F32) for m in CUT],
            [vmem((n, VECS, m, B), F32) for m in CUT],
            vmem((PARTS, 4 * max(CUT), 128), F32),
            vmem((Z - 1, 8, 128), F32),
            dma((6,)),
            dma((2, VECS)),
            dma((2, VECS)),
            dma((PARTS,)),
            dma((PARTS,)),
            dma((2,)),
            pltpu.SemaphoreType.REGULAR((5,)),
        ],
        compiler_params=pltpu.CompilerParams(
            collective_id=0, has_side_effects=True, vmem_limit_bytes=56 << 20
        ),
        cost_estimate=pl.CostEstimate(flops=3 * 2**30, bytes_accessed=9 << 19, transcendentals=0),
    )(term_shift, term_count, sector_dims,
      wavefunction.reshape(VECS, B, B), left_ops.reshape(KT, B, B), right_ops.reshape(KT, B, B))
    return out.reshape(VECS, 2, 2, 128).transpose(0, 2, 1, 3).reshape(VECS, 1, 2, B)


def solution(mesh):
    in_specs = (
        P(None, "sec", None, None),
        P("op", "sec", None, None),
        P("op", "sec", None, None),
        P("op"),
        P("op"),
        P("sec"),
    )
    out_specs = P(None, "sec", "op", None)
    return jax.shard_map(shards, mesh=mesh, in_specs=in_specs, out_specs=out_specs, check_vma=False)
```

```python
import jax
import jax.numpy as jnp
from jax import lax
from jax.experimental import pallas as pl
from jax.experimental.pallas import tpu as pltpu
from jax.sharding import PartitionSpec as P

MESH = pl.DeviceIdType.MESH
F32, BF16 = jnp.float32, jnp.bfloat16
XH, Y, Z = 2, 4, 16
VECS, B, KT = 2, 256, 8
HUB = 4
ENDS = (0, 4, 8, 16)
PARTS = len(ENDS) - 1
CUT = [2 * (b - a) for a, b in zip(ENDS, ENDS[1:])]
ROWS = [XH * Y * n for n in CUT]
NEAR = [(a, b) for a in range(XH) for b in range(Y) if (a, b) != (0, 0)]
NN = (((1,), (0,)), ((), ()))


def split(x):
    hi = x.astype(BF16)
    return hi, (x - hi.astype(F32)).astype(BF16)


def dot(a, b, dims):
    return lax.dot_general(a, b, dims, preferred_element_type=F32)


def kernel(
    shift_hbm, count_hbm, dims_hbm, w_hbm, l_hbm, r_hbm, out_ref,
    shift_ref, count_ref, dims_ref, wv, lv, rv, got, sh, sl, ls, rh, rl, gs, part, near_buf, zsrc, zbuf,
    load_sem, own_sem, ex_send, ex_recv, near_send, near_recv, z_sem, know,
):
    op, sec = lax.axis_index("op"), lax.axis_index("sec")
    xh, y, z = op // (Y * Z), (op // Z) % Y, op % Z

    def place(a, b, c):
        return (a * (Y * Z) + b * Z + c, sec)

    def signal(sem, target):
        pl.semaphore_signal(sem, inc=1, device_id=target, device_id_type=MESH)

    loads = [
        pltpu.make_async_copy(s, d, load_sem.at[i])
        for i, (s, d) in enumerate(
            ((dims_hbm, dims_ref), (w_hbm, wv), (l_hbm, lv), (r_hbm, rv), (shift_hbm, shift_ref), (count_hbm, count_ref))
        )
    ]
    quarter = B // 2
    own = [
        pltpu.make_async_copy(w_hbm.at[v, pl.ds(h * quarter, quarter)], wv.at[v, pl.ds(h * quarter, quarter)], own_sem.at[v, h])
        for v in range(VECS)
        for h in range(2)
    ]
    for c in own:
        c.start()
    loads[0].start()

    barrier = pltpu.get_barrier_semaphore()
    other_op = (1 - xh) * (Y * Z) + y * Z + z
    up = jnp.where(sec < 3, sec + 1, sec - 3)
    down = jnp.where(sec > 0, sec - 1, sec + 3)
    for a in (op, other_op):
        signal(barrier, (a, up))
        signal(barrier, (a, down))
    beside = [place(xh, (y + d) % Y, z) for d in (1, 3)]
    for target in beside:
        signal(barrier, target)

    @pl.when(z < HUB)
    def _():
        for d in range(1, Z):

            @pl.when(z + d < Z)
            def _():
                signal(barrier, place(xh, y, (z + d) % Z))

    loads[0].wait()
    rows = dims_ref[0]
    row = lax.broadcasted_iota(jnp.int32, (B, B), 0)
    for v in range(VECS):
        own[2 * v].wait()
        own[2 * v + 1].wait()
        wv[v] = jnp.where(row < rows, wv[v], 0.0)
    pl.semaphore_wait(barrier, 6 + jnp.where(z < HUB, z, HUB))

    def arrived(ref, sem):
        pltpu.make_async_copy(ref, ref, sem).wait()

    def ways(step):
        cross = (sec == 1) if step == 0 else (sec == 2)
        target = sec + 1 if step == 0 else sec - 1
        second = jnp.where(cross, other_op, op)
        slot = 0 if step == 0 else 1
        copies = []
        for v in range(VECS):
            for half in range(2):
                part_rows = pl.ds(half * (B // 2), B // 2)
                copies.append(
                    pltpu.make_async_remote_copy(
                        src_ref=wv.at[v, part_rows],
                        dst_ref=got.at[slot, v, part_rows],
                        send_sem=ex_send.at[slot, v],
                        recv_sem=ex_recv.at[slot, v],
                        device_id=(op if half == 0 else second, target),
                        device_id_type=MESH,
                    )
                )
        return copies

    to_next, to_prev = ways(0), ways(1)

    @pl.when(sec < 3)
    def _():
        for c in to_next:
            c.start()

    @pl.when(sec > 0)
    def _():
        for c in to_prev:
            c.start()

    for i in (2, 3, 4, 5):
        loads[i].start()

    for target in beside:
        signal(know.at[0], target)
    for d in range(HUB):

        @pl.when(z >= HUB)
        def _():
            signal(know.at[1], place(xh, y, d))

        @pl.when((z < HUB) & (d < z))
        def _():
            signal(know.at[2], place(xh, y, d))

    for v in range(VECS):
        h, l = split(wv[v])
        sh[v, 1] = h
        sl[v, 1] = l
        sh[v, 3] = jnp.zeros((B, B), BF16)
        sl[v, 3] = jnp.zeros((B, B), BF16)

    loads[2].wait()

    def split_l(t, carry):
        x = lv[t].reshape(XH * Y, 2 * Z, B)
        for c in range(PARTS):
            h, l = split(x[:, 2 * ENDS[c] : 2 * ENDS[c + 1]].reshape(ROWS[c], B))
            ls[c][t, : ROWS[c]] = h
            ls[c][t, ROWS[c] :] = l
        return carry

    lax.fori_loop(0, KT, split_l, 0)
    loads[3].wait()
    for t in range(KT):
        h, l = split(rv[t].T)
        rh[t] = h
        rl[t] = l

    loads[4].wait()
    loads[5].wait()
    index = []
    for t in range(KT):
        s = shift_ref[t]
        at = sec - s
        ok = (t < count_ref[0]) & (at >= 0) & (at <= 3)
        index.append(jnp.where(ok, 1 - s, 3))

    def slab(c, v, i):
        return (v, i) if c == 0 else (i, v)

    def left(c, v):
        m = ROWS[c]
        for t in range(KT):
            i = index[t]
            g = dot(ls[c][t], sh[v, i], NN)
            h, l = split(g[:m] + g[m:] + dot(ls[c][t, :m], sl[v, i], NN))
            gs[c][(*slab(c, v, 0), slice(None), slice(t * B, (t + 1) * B))] = h
            gs[c][(*slab(c, v, 1), slice(None), slice(t * B, (t + 1) * B))] = l

    def right(c, vs):
        n = len(vs) * ROWS[c]
        both = gs[c][vs[0]] if len(vs) == 1 else gs[c][...]
        p = dot(both.reshape(2 * n, KT * B), rh[...].reshape(KT * B, B), NN)
        p = p[:n] + p[n:] + dot(both[0].reshape(n, KT * B), rl[...].reshape(KT * B, B), NN)
        p = p.reshape(len(vs), XH * Y, CUT[c], B)
        for k, v in enumerate(vs):
            for q in range(XH * Y):
                part[c][q, v] = p[k, q]

    for v in range(VECS):
        for edge, slot, i in ((sec > 0, 0, 0), (sec < 3, 1, 2)):

            @pl.when(edge)
            def _():
                arrived(got.at[slot, v], ex_recv.at[slot, v])
                h, l = split(got[slot, v])
                sh[v, i] = h
                sl[v, i] = l

        if v == 0:
            pl.semaphore_wait(know.at[0], 2)
            for d in (1, 2, 3):
                signal(know.at[3], place(xh, (y + d) % Y, z))
        left(0, v)
        right(0, (v,))

    def near_copy(c, a, b):
        i = NEAR.index((a, b))
        to = (xh + a) % XH * Y + (y + b) % Y
        return pltpu.make_async_remote_copy(
            src_ref=part[c].at[to],
            dst_ref=near_buf[c].at[i],
            send_sem=near_send.at[c],
            recv_sem=near_recv.at[c],
            device_id=(to * Z + z, sec),
            device_id_type=MESH,
        )

    near = [[near_copy(c, a, b) for a, b in NEAR] for c in range(PARTS)]
    for c in range(PARTS):
        if c > 0:
            for v in range(VECS):
                left(c, v)
            right(c, (0, 1))
        if c == 0:
            pl.semaphore_wait(know.at[3], 3)
        for a, b in ((1, 2), (1, 1), (1, 3), (1, 0), (0, 2), (0, 1), (0, 3)):
            near[c][NEAR.index((a, b))].start()

    def far_copy(c, j):
        to = ENDS[c] + j
        slot = (to - z + Z) % Z - 1
        slot = jnp.where(slot < 0, 0, slot)
        return pltpu.make_async_remote_copy(
            src_ref=zsrc.at[c, pl.ds(j * 8, 8)],
            dst_ref=zbuf.at[slot],
            send_sem=z_sem.at[0],
            recv_sem=z_sem.at[1],
            device_id=place(xh, y, to),
            device_id_type=MESH,
        )

    for c in range(PARTS):
        arrived(near_buf[c], near_recv.at[c])
        total = part[c][xh * Y + y]
        for i in range(len(NEAR)):
            total = total + near_buf[c][i]
        for v in range(VECS):
            for rb in range(CUT[c] // 8):
                for ch in range(2):
                    zsrc[c, pl.ds(32 * rb + 2 * v + ch, 8, stride=4), :] = total[
                        v, rb * 8 : rb * 8 + 8, ch * 128 : ch * 128 + 128
                    ]
        if c == 0:

            @pl.when(z < HUB - 1)
            def _():
                pl.semaphore_wait(know.at[2], HUB - 1 - z)

        if c == 1:

            @pl.when(z < HUB)
            def _():
                pl.semaphore_wait(know.at[1], Z - HUB)
                for d in range(HUB, Z, HUB):
                    signal(know.at[4], place(xh, y, z + d))

            @pl.when(z >= HUB)
            def _():
                pl.semaphore_wait(know.at[4], 1)

        for j in range(ENDS[c + 1] - ENDS[c]):

            @pl.when(ENDS[c] + j != z)
            def _():
                far_copy(c, j).start()

    @pl.when(sec < 3)
    def _():
        for v in range(VECS):
            arrived(wv.at[v], ex_send.at[0, v])

    @pl.when(sec > 0)
    def _():
        for v in range(VECS):
            arrived(wv.at[v], ex_send.at[1, v])

    for c in range(PARTS):
        arrived(near_buf[c], near_send.at[c])
    arrived(zbuf, z_sem.at[0])

    mine, first = 0, 0
    for c in range(1, PARTS):
        mine = jnp.where(z >= ENDS[c], c, mine)
        first = jnp.where(z >= ENDS[c], ENDS[c], first)
    tile = zsrc[mine, pl.ds(pl.multiple_of((z - first) * 8, 8), 8)]
    sub = lax.broadcasted_iota(jnp.int32, (8, 128), 0)
    own_row = 2 * op + jnp.where(sub >= 4, 1, 0)
    arrived(zbuf, z_sem.at[1])
    for k in range(Z - 1):
        tile = tile + zbuf[k]
    tile = jnp.where(own_row < rows, tile, 0.0)
    for s in range(2):
        out_ref[pl.ds(s, 4, stride=2), :] = tile[4 * s : 4 * s + 4]


def shards(wavefunction, left_ops, right_ops, term_shift, term_count, sector_dims):
    vmem, smem, dma = pltpu.VMEM, pltpu.SMEM, pltpu.SemaphoreType.DMA
    n = len(NEAR)
    out = pl.pallas_call(
        kernel,
        out_shape=vmem((8, 128), F32),
        in_specs=[pl.BlockSpec(memory_space=pltpu.HBM)] * 3 + [pl.BlockSpec(memory_space=pl.ANY)] * 3,
        out_specs=pl.BlockSpec(memory_space=vmem),
        scratch_shapes=[
            smem((KT,), jnp.int32),
            smem((1,), jnp.int32),
            smem((1,), jnp.int32),
            vmem((VECS, B, B), F32),
            vmem((KT, B, B), F32),
            vmem((KT, B, B), F32),
            vmem((2, VECS, B, B), F32),
            vmem((VECS, 4, B, B), BF16),
            vmem((VECS, 4, B, B), BF16),
            [vmem((KT, 2 * m, B), BF16) for m in ROWS],
            vmem((KT, B, B), BF16),
            vmem((KT, B, B), BF16),
            [vmem((2, 2, m, KT * B), BF16) for m in ROWS],
            [vmem((XH * Y, VECS, m, B), F32) for m in CUT],
            [vmem((n, VECS, m, B), F32) for m in CUT],
            vmem((PARTS, 4 * max(CUT), 128), F32),
            vmem((Z - 1, 8, 128), F32),
            dma((6,)),
            dma((VECS, 2)),
            dma((2, VECS)),
            dma((2, VECS)),
            dma((PARTS,)),
            dma((PARTS,)),
            dma((2,)),
            pltpu.SemaphoreType.REGULAR((5,)),
        ],
        compiler_params=pltpu.CompilerParams(
            collective_id=0, has_side_effects=True, vmem_limit_bytes=56 << 20
        ),
        cost_estimate=pl.CostEstimate(flops=3 * 2**30, bytes_accessed=9 << 19, transcendentals=0),
    )(term_shift, term_count, sector_dims,
      wavefunction.reshape(VECS, B, B), left_ops.reshape(KT, B, B), right_ops.reshape(KT, B, B))
    return out.reshape(VECS, 2, 2, 128).transpose(0, 2, 1, 3).reshape(VECS, 1, 2, B)


def solution(mesh):
    in_specs = (
        P(None, "sec", None, None),
        P("op", "sec", None, None),
        P("op", "sec", None, None),
        P("op"),
        P("op"),
        P("sec"),
    )
    out_specs = P(None, "sec", "op", None)
    return jax.shard_map(shards, mesh=mesh, in_specs=in_specs, out_specs=out_specs, check_vma=False)
```

```python
import jax
import jax.numpy as jnp
from jax import lax
from jax.experimental import pallas as pl
from jax.experimental.pallas import tpu as pltpu
from jax.sharding import PartitionSpec as P

MESH = pl.DeviceIdType.MESH
F32, BF16 = jnp.float32, jnp.bfloat16
XH, Y, Z = 2, 4, 16
VECS, B, KT = 2, 256, 8
HUB = 4
ENDS = (0, 4, 8, 16)
PARTS = len(ENDS) - 1
CUT = [2 * (b - a) for a, b in zip(ENDS, ENDS[1:])]
ROWS = [XH * Y * n for n in CUT]
NEAR = [(a, b) for a in range(XH) for b in range(Y) if (a, b) != (0, 0)]
NN = (((1,), (0,)), ((), ()))


def split(x):
    hi = x.astype(BF16)
    return hi, (x - hi.astype(F32)).astype(BF16)


def dot(a, b, dims):
    return lax.dot_general(a, b, dims, preferred_element_type=F32)


def kernel(
    shift_hbm, count_hbm, dims_hbm, w_hbm, l_hbm, r_hbm, out_ref,
    shift_ref, count_ref, dims_ref, wv, lv, rv, got, sh, sl, ls, rh, rl, gs, part, near_buf, zsrc, zbuf,
    load_sem, ex_send, ex_recv, near_send, near_recv, z_sem, know,
):
    op, sec = lax.axis_index("op"), lax.axis_index("sec")
    xh, y, z = op // (Y * Z), (op // Z) % Y, op % Z

    def place(a, b, c):
        return (a * (Y * Z) + b * Z + c, sec)

    def signal(sem, target):
        pl.semaphore_signal(sem, inc=1, device_id=target, device_id_type=MESH)

    loads = [
        pltpu.make_async_copy(s, d, load_sem.at[i])
        for i, (s, d) in enumerate(
            ((dims_hbm, dims_ref), (w_hbm, wv), (l_hbm, lv), (r_hbm, rv), (shift_hbm, shift_ref), (count_hbm, count_ref))
        )
    ]
    loads[0].start()
    loads[1].start()

    barrier = pltpu.get_barrier_semaphore()
    other_op = (1 - xh) * (Y * Z) + y * Z + z
    up = jnp.where(sec < 3, sec + 1, sec - 3)
    down = jnp.where(sec > 0, sec - 1, sec + 3)
    for a in (op, other_op):
        signal(barrier, (a, up))
        signal(barrier, (a, down))
    beside = [place(xh, (y + d) % Y, z) for d in (1, 3)]
    for target in beside:
        signal(barrier, target)

    @pl.when(z < HUB)
    def _():
        for d in range(1, Z):

            @pl.when(z + d < Z)
            def _():
                signal(barrier, place(xh, y, (z + d) % Z))

    loads[0].wait()
    loads[1].wait()
    rows = dims_ref[0]
    row = lax.broadcasted_iota(jnp.int32, (B, B), 0)
    for v in range(VECS):
        wv[v] = jnp.where(row < rows, wv[v], 0.0)
    for i in (2, 3, 4, 5):
        loads[i].start()
    pl.semaphore_wait(barrier, 6 + jnp.where(z < HUB, z, HUB))

    def arrived(ref, sem):
        pltpu.make_async_copy(ref, ref, sem).wait()

    def ways(step):
        cross = (sec == 1) if step == 0 else (sec == 2)
        target = sec + 1 if step == 0 else sec - 1
        second = jnp.where(cross, other_op, op)
        slot = 0 if step == 0 else 1
        copies = []
        for v in range(VECS):
            for half in range(2):
                part_rows = pl.ds(half * (B // 2), B // 2)
                copies.append(
                    pltpu.make_async_remote_copy(
                        src_ref=wv.at[v, part_rows],
                        dst_ref=got.at[slot, v, part_rows],
                        send_sem=ex_send.at[slot, v],
                        recv_sem=ex_recv.at[slot, v],
                        device_id=(op if half == 0 else second, target),
                        device_id_type=MESH,
                    )
                )
        return copies

    to_next, to_prev = ways(0), ways(1)

    @pl.when(sec < 3)
    def _():
        for c in to_next:
            c.start()

    @pl.when(sec > 0)
    def _():
        for c in to_prev:
            c.start()

    for target in beside:
        signal(know.at[0], target)
    for d in range(HUB):

        @pl.when(z >= HUB)
        def _():
            signal(know.at[1], place(xh, y, d))

        @pl.when((z < HUB) & (d < z))
        def _():
            signal(know.at[2], place(xh, y, d))

    for v in range(VECS):
        h, l = split(wv[v])
        sh[v, 1] = h
        sl[v, 1] = l
        sh[v, 3] = jnp.zeros((B, B), BF16)
        sl[v, 3] = jnp.zeros((B, B), BF16)

    loads[2].wait()

    def split_l(t, carry):
        x = lv[t].reshape(XH * Y, 2 * Z, B)
        for c in range(PARTS):
            h, l = split(x[:, 2 * ENDS[c] : 2 * ENDS[c + 1]].reshape(ROWS[c], B))
            ls[c][t, : ROWS[c]] = h
            ls[c][t, ROWS[c] :] = l
        return carry

    lax.fori_loop(0, KT, split_l, 0)
    loads[3].wait()
    for t in range(KT):
        h, l = split(rv[t].T)
        rh[t] = h
        rl[t] = l

    loads[4].wait()
    loads[5].wait()
    index = []
    for t in range(KT):
        s = shift_ref[t]
        at = sec - s
        ok = (t < count_ref[0]) & (at >= 0) & (at <= 3)
        index.append(jnp.where(ok, 1 - s, 3))

    def slab(c, v, i):
        return (v, i) if c == 0 else (i, v)

    def left(c, v):
        m = ROWS[c]
        for t in range(KT):
            i = index[t]
            g = dot(ls[c][t], sh[v, i], NN)
            h, l = split(g[:m] + g[m:] + dot(ls[c][t, :m], sl[v, i], NN))
            gs[c][(*slab(c, v, 0), slice(None), slice(t * B, (t + 1) * B))] = h
            gs[c][(*slab(c, v, 1), slice(None), slice(t * B, (t + 1) * B))] = l

    def right(c, vs):
        n = len(vs) * ROWS[c]
        both = gs[c][vs[0]] if len(vs) == 1 else gs[c][...]
        p = dot(both.reshape(2 * n, KT * B), rh[...].reshape(KT * B, B), NN)
        p = p[:n] + p[n:] + dot(both[0].reshape(n, KT * B), rl[...].reshape(KT * B, B), NN)
        p = p.reshape(len(vs), XH * Y, CUT[c], B)
        for k, v in enumerate(vs):
            for q in range(XH * Y):
                part[c][q, v] = p[k, q]

    for v in range(VECS):
        for edge, slot, i in ((sec > 0, 0, 0), (sec < 3, 1, 2)):

            @pl.when(edge)
            def _():
                arrived(got.at[slot, v], ex_recv.at[slot, v])
                h, l = split(got[slot, v])
                sh[v, i] = h
                sl[v, i] = l

        if v == 0:
            pl.semaphore_wait(know.at[0], 2)
            for d in (1, 2, 3):
                signal(know.at[3], place(xh, (y + d) % Y, z))
        left(0, v)
        right(0, (v,))

    def near_copy(c, a, b):
        i = NEAR.index((a, b))
        to = (xh + a) % XH * Y + (y + b) % Y
        return pltpu.make_async_remote_copy(
            src_ref=part[c].at[to],
            dst_ref=near_buf[c].at[i],
            send_sem=near_send.at[c],
            recv_sem=near_recv.at[c],
            device_id=(to * Z + z, sec),
            device_id_type=MESH,
        )

    near = [[near_copy(c, a, b) for a, b in NEAR] for c in range(PARTS)]

    def make(c):
        if c > 0:
            for v in range(VECS):
                left(c, v)
            right(c, (0, 1))
        if c == 0:
            pl.semaphore_wait(know.at[3], 3)
        for a, b in ((1, 2), (1, 1), (1, 3), (1, 0), (0, 2), (0, 1), (0, 3)):
            near[c][NEAR.index((a, b))].start()

    def far_copy(c, j):
        to = ENDS[c] + j
        slot = (to - z + Z) % Z - 1
        slot = jnp.where(slot < 0, 0, slot)
        return pltpu.make_async_remote_copy(
            src_ref=zsrc.at[c, pl.ds(j * 8, 8)],
            dst_ref=zbuf.at[slot],
            send_sem=z_sem.at[0],
            recv_sem=z_sem.at[1],
            device_id=place(xh, y, to),
            device_id_type=MESH,
        )

    def onward(c):
        arrived(near_buf[c], near_recv.at[c])
        total = part[c][xh * Y + y]
        for i in range(len(NEAR)):
            total = total + near_buf[c][i]
        for v in range(VECS):
            for rb in range(CUT[c] // 8):
                for ch in range(2):
                    zsrc[c, pl.ds(32 * rb + 2 * v + ch, 8, stride=4), :] = total[
                        v, rb * 8 : rb * 8 + 8, ch * 128 : ch * 128 + 128
                    ]
        if c == 0:

            @pl.when(z < HUB - 1)
            def _():
                pl.semaphore_wait(know.at[2], HUB - 1 - z)

        if c == 1:

            @pl.when(z < HUB)
            def _():
                pl.semaphore_wait(know.at[1], Z - HUB)
                for d in range(HUB, Z, HUB):
                    signal(know.at[4], place(xh, y, z + d))

            @pl.when(z >= HUB)
            def _():
                pl.semaphore_wait(know.at[4], 1)

        for j in range(ENDS[c + 1] - ENDS[c]):

            @pl.when(ENDS[c] + j != z)
            def _():
                far_copy(c, j).start()

    make(0)
    make(1)
    onward(0)
    make(2)
    onward(1)
    onward(2)

    @pl.when(sec < 3)
    def _():
        for v in range(VECS):
            arrived(wv.at[v], ex_send.at[0, v])

    @pl.when(sec > 0)
    def _():
        for v in range(VECS):
            arrived(wv.at[v], ex_send.at[1, v])

    for c in range(PARTS):
        arrived(near_buf[c], near_send.at[c])
    arrived(zbuf, z_sem.at[0])

    mine, first = 0, 0
    for c in range(1, PARTS):
        mine = jnp.where(z >= ENDS[c], c, mine)
        first = jnp.where(z >= ENDS[c], ENDS[c], first)
    tile = zsrc[mine, pl.ds(pl.multiple_of((z - first) * 8, 8), 8)]
    sub = lax.broadcasted_iota(jnp.int32, (8, 128), 0)
    own_row = 2 * op + jnp.where(sub >= 4, 1, 0)
    arrived(zbuf, z_sem.at[1])
    for k in range(Z - 1):
        tile = tile + zbuf[k]
    tile = jnp.where(own_row < rows, tile, 0.0)
    for s in range(2):
        out_ref[pl.ds(s, 4, stride=2), :] = tile[4 * s : 4 * s + 4]


def shards(wavefunction, left_ops, right_ops, term_shift, term_count, sector_dims):
    vmem, smem, dma = pltpu.VMEM, pltpu.SMEM, pltpu.SemaphoreType.DMA
    n = len(NEAR)
    out = pl.pallas_call(
        kernel,
        out_shape=vmem((8, 128), F32),
        in_specs=[pl.BlockSpec(memory_space=pltpu.HBM)] * 3 + [pl.BlockSpec(memory_space=pl.ANY)] * 3,
        out_specs=pl.BlockSpec(memory_space=vmem),
        scratch_shapes=[
            smem((KT,), jnp.int32),
            smem((1,), jnp.int32),
            smem((1,), jnp.int32),
            vmem((VECS, B, B), F32),
            vmem((KT, B, B), F32),
            vmem((KT, B, B), F32),
            vmem((2, VECS, B, B), F32),
            vmem((VECS, 4, B, B), BF16),
            vmem((VECS, 4, B, B), BF16),
            [vmem((KT, 2 * m, B), BF16) for m in ROWS],
            vmem((KT, B, B), BF16),
            vmem((KT, B, B), BF16),
            [vmem((2, 2, m, KT * B), BF16) for m in ROWS],
            [vmem((XH * Y, VECS, m, B), F32) for m in CUT],
            [vmem((n, VECS, m, B), F32) for m in CUT],
            vmem((PARTS, 4 * max(CUT), 128), F32),
            vmem((Z - 1, 8, 128), F32),
            dma((6,)),
            dma((2, VECS)),
            dma((2, VECS)),
            dma((PARTS,)),
            dma((PARTS,)),
            dma((2,)),
            pltpu.SemaphoreType.REGULAR((5,)),
        ],
        compiler_params=pltpu.CompilerParams(
            collective_id=0, has_side_effects=True, vmem_limit_bytes=56 << 20
        ),
        cost_estimate=pl.CostEstimate(flops=3 * 2**30, bytes_accessed=9 << 19, transcendentals=0),
    )(term_shift, term_count, sector_dims,
      wavefunction.reshape(VECS, B, B), left_ops.reshape(KT, B, B), right_ops.reshape(KT, B, B))
    return out.reshape(VECS, 2, 2, 128).transpose(0, 2, 1, 3).reshape(VECS, 1, 2, B)


def solution(mesh):
    in_specs = (
        P(None, "sec", None, None),
        P("op", "sec", None, None),
        P("op", "sec", None, None),
        P("op"),
        P("op"),
        P("sec"),
    )
    out_specs = P(None, "sec", "op", None)
    return jax.shard_map(shards, mesh=mesh, in_specs=in_specs, out_specs=out_specs, check_vma=False)
```
